32 devices in a mesh: scen: 8 (over z, y), blk: 4 (over x, core).
Axes of the slice: x: 2, y: 2, z: 4, core: 2. Of those that a mesh axis runs over, the one named last changes fastest.
Arguments:
- draws: bfloat16 [2048, 8192], P('blk', 'scen'), may hold values from -6 to 6
- factor: bfloat16 [8192, 8192], P('scen', 'blk'), may hold values from -0.1875 to 0.1875
- occupancy: int32 [16, 16], replicated, may hold values from 0 to 1, as said below
Outputs:
- scenarios: bfloat16 [2048, 8192], P('blk', 'scen')
The draws below stay inside these ranges and needn't reach their ends.
Inputs may be any that keep to these rules, and one draw needn't show every extreme that they name: occupancy[i, i] is 1 for every i, occupancy[i, j] is 0 for j > i, and each entry below the diagonal is 0 or 1.
All inputs are finite; a program needn't handle non-finite values.
Results may differ from the reference program's by a relative error of at most 0.001.
Values may be sent and summed in bfloat16 or wider, within the bound.
A program may use at most 64 MiB of HBM per device.

```python
import jax
import jax.numpy as jnp

FACTORS = 8192
TILE = 512
SCENARIOS = 2048
TILES = 16


def draw_occupancy(key, part):
    bits = jax.random.randint(key, (TILES, TILES), 0, 2, dtype=jnp.int32)
    rows = jnp.arange(TILES, dtype=jnp.int32)[:, None]
    cols = jnp.arange(TILES, dtype=jnp.int32)[None, :]
    lower = jnp.where(cols < rows, bits, jnp.zeros_like(bits))
    return jnp.where(rows == cols, jnp.ones_like(bits), lower).astype(jnp.int32)


def steps_of(key, dims, pieces, least, largest):
    def one(axis_at, parts):
        steps = jax.random.uniform(jax.random.fold_in(jax.random.fold_in(key, 6), axis_at), (parts,), jnp.float32, least / len(pieces), largest / len(pieces))
        return jnp.repeat(jnp.exp(steps), dims[axis_at] // parts).reshape((-1,) + (1,) * (len(dims) - axis_at - 1))

    level = one(*pieces[0])
    for cut in pieces[1:]:
        level = level * one(*cut)
    return level


def gaussian(stream_key, extent, spread, most, split=(), kind=jnp.bfloat16):
    gain = steps_of(stream_key, extent, split, -0.22, 0.18) if split else 1.0
    drawn = jax.random.normal(stream_key, extent, jnp.float32) * spread * gain
    return jnp.minimum(jnp.maximum(drawn, -most), most).astype(kind)


def setup_inputs(seed: int = 0) -> dict:
    seeds = jax.random.split(jax.random.key(seed), 4)
    return {
        "draws": gaussian(seeds[0], (SCENARIOS, FACTORS), 1.0, 6.0, ((0, 4), (1, 8))),
        "factor": gaussian(seeds[1], (FACTORS, FACTORS), (2 * TILE) ** -0.5, 0.1875, ((0, 8), (1, 4))),
        "occupancy": draw_occupancy(jax.random.fold_in(seeds[3], 71), 0),
    }


def reference(draws, factor, occupancy):
    width = factor.shape[0]
    occ_full = jnp.repeat(jnp.repeat(occupancy, TILE, axis=0), TILE, axis=1)
    rows = jnp.arange(width, dtype=jnp.int32)[:, None]
    cols = jnp.arange(width, dtype=jnp.int32)[None, :]
    keep = (occ_full == 1) & (cols <= rows)
    used = jnp.where(keep, factor, jnp.zeros((), factor.dtype))
    return jnp.dot(draws, used.T, preferred_element_type=jnp.float32).astype(jnp.bfloat16)
```

```python
import functools

import jax
import jax.numpy as jnp
from jax import lax
from jax.experimental import pallas as pl
from jax.experimental.pallas import tpu as pltpu
from jax.sharding import PartitionSpec as P

MESH = pl.DeviceIdType.MESH


def kernel(
    tile, scens, blks,
    draws, factor, occ, out,
    dbuf, fbuf, acc,
    zsend, zrecv, ysend, yrecv, xsend, xrecv, csend, crecv, dload, fload,
):
    levels, groups = scens // 2, blks // 2
    rows, cols = factor.shape
    rt_n, ct_n = rows // tile, cols // tile
    half = draws.shape[0] // 2
    z_n = levels * rt_n
    f_n = rt_n * ct_n
    x_n = (groups - 1) * f_n
    k = lax.axis_index("scen")
    b = lax.axis_index("blk")
    z, y = k // 2, k % 2
    x, c = b // 2, b % 2

    def d_tile(n, col):
        return ((z - n // rt_n) * 2 + col) * rt_n + n % rt_n

    def d_has(n, col):
        lev = z - n // rt_n
        return (n >= 0) & (n < z_n) & (lev >= 0) & (lev * 2 + col <= k)

    def when(inside, cond, body):
        if inside:
            pl.when(cond())(body)

    def z_copy(n, recv):
        t = d_tile(n, y)
        i = n if recv else n + rt_n
        return pltpu.make_async_remote_copy(
            src_ref=dbuf.at[t], dst_ref=dbuf.at[t],
            send_sem=zsend.at[n], recv_sem=zrecv.at[i],
            device_id=(k + 2, b), device_id_type=MESH,
        )

    def y_copy(n, recv):
        t = d_tile(n, 1 - y if recv else y)
        return pltpu.make_async_remote_copy(
            src_ref=dbuf.at[t], dst_ref=dbuf.at[t],
            send_sem=ysend.at[n], recv_sem=yrecv.at[n],
            device_id=(z * 2 + 1 - y, b), device_id_type=MESH,
        )

    def y_sends(n):
        return d_has(n, y) & ((y == 0) | (n >= rt_n))

    def f_at(owner, f):
        return owner * ct_n + (ct_n - 1 - f // rt_n), f % rt_n

    def f_has(owner, f):
        t, r = f_at(owner, f)
        return t <= k * rt_n + r

    def x_owner(m, sending):
        step = m // f_n + 1
        other = lax.rem(x + step, groups) if sending else lax.rem(x + groups - step, groups)
        return other * 2 + c

    def x_copy(m, sending):
        f = m % f_n
        peer = x_owner(m, sending)
        t, r = f_at(b if sending else peer, f)
        return pltpu.make_async_remote_copy(
            src_ref=fbuf.at[t, r], dst_ref=fbuf.at[t, r],
            send_sem=xsend.at[m], recv_sem=xrecv.at[m],
            device_id=(k, peer), device_id_type=MESH,
        )

    def x_has(m, sending):
        return (m >= 0) & (m < x_n) & f_has(b if sending else x_owner(m, sending), m % f_n)

    def c_owner(q, core):
        m = q - f_n
        step = m // f_n + 1
        other = lax.rem(x + groups - step, groups)
        return jnp.where(q < f_n, x, other) * 2 + core

    def c_copy(q, core):
        t, r = f_at(c_owner(q, core), q % f_n)
        return pltpu.make_async_remote_copy(
            src_ref=fbuf.at[t, r], dst_ref=fbuf.at[t, r],
            send_sem=csend.at[q], recv_sem=crecv.at[q],
            device_id=(k, x * 2 + 1 - c), device_id_type=MESH,
        )

    def c_has(q, core):
        return (q >= 0) & (q < f_n + x_n) & f_has(c_owner(q, core), q % f_n)

    def d_load(h):
        return pltpu.make_async_copy(
            draws.at[:, pl.ds(h * tile, tile)], dbuf.at[k * rt_n + h], dload.at[h]
        )

    def f_load(f):
        t, r = f_at(b, f)
        lt = ct_n - 1 - f // rt_n
        return pltpu.make_async_copy(
            factor.at[pl.ds(r * tile, tile), pl.ds(lt * tile, tile)],
            fbuf.at[t, r],
            fload.at[f],
        )

    for h in range(rt_n):
        d_load(h).start()

    def load_f(f):
        @pl.when(f_has(b, f))
        def _():
            f_load(f).start()

    for f in range(f_n):
        load_f(f)

    barrier = pltpu.get_barrier_semaphore()

    def greet(kk, bb):
        pl.semaphore_signal(barrier, inc=1, device_id=(kk, bb), device_id_type=MESH)

    greet(z * 2 + 1 - y, b)
    greet(k, x * 2 + 1 - c)
    for step in range(1, groups):
        greet(k, lax.rem(x + step, groups) * 2 + c)

    @pl.when(z > 0)
    def _():
        greet(k - 2, b)

    @pl.when(z < levels - 1)
    def _():
        greet(k + 2, b)

    ends = jnp.where(z > 0, 1, 0) + jnp.where(z < levels - 1, 1, 0)
    pl.semaphore_wait(barrier, groups + 1 + ends)

    def forward_d(n):
        if n + rt_n < z_n:
            pl.when(z < levels - 1)(lambda: z_copy(n, False).start())
        pl.when(y_sends(n))(lambda: y_copy(n, False).start())

    def send_x(m):
        when(0 <= m < x_n, lambda: x_has(m, True), lambda: x_copy(m, True).start())

    for h in range(rt_n):
        d_load(h).wait()
        forward_d(h)

    def wait_f(f):
        @pl.when(f_has(b, f))
        def _():
            f_load(f).wait()

    for f in range(f_n):
        wait_f(f)
    send_x(0)
    send_x(1)

    def give_own(q):
        pl.when(c_has(q, c))(lambda: c_copy(q, c).start())

    for q in range(f_n):
        give_own(q)

    acc[...] = jnp.zeros_like(acc)

    def d_tick(t):
        owner, h = t // rt_n, t % rt_n
        lev, col = owner // 2, owner % 2
        n = (z - lev) * rt_n + h
        same = jnp.where(lev == z, 0, n - rt_n + 1)
        return jnp.where(col == y, same, n + 1)

    def f_tick(t, r):
        owner = t // ct_n
        f = (ct_n - 1 - t % ct_n) * rt_n + r
        ox, oc = owner // 2, owner % 2
        m = (lax.rem(x - ox + groups, groups) - 1) * f_n + f
        near = jnp.where(oc == c, 0, 1)
        far = jnp.where(oc == c, m + 1, m + 2)
        return jnp.where(ox == x, near, far)

    def product(t, r, masked):
        block = fbuf[t, r]
        if masked:
            row = lax.broadcasted_iota(jnp.int32, block.shape, 0)
            col = lax.broadcasted_iota(jnp.int32, block.shape, 1)
            block = jnp.where(col <= row, block.astype(jnp.float32), 0.0).astype(block.dtype)
        at_row = lax.broadcasted_iota(jnp.int32, occ.shape, 0) == k * rt_n + r
        at_col = lax.broadcasted_iota(jnp.int32, occ.shape, 1) == t
        mark = jnp.where(at_row & at_col, occ[...].astype(jnp.float32), 0.0)
        on = jnp.sum(jnp.sum(mark, axis=1, keepdims=True), axis=0, keepdims=True)
        for s in range(0, draws.shape[0], half):
            part = lax.dot_general(
                dbuf[t, s:s + half], block, (((1,), (1,)), ((), ())),
                preferred_element_type=jnp.float32,
            )
            acc[r, s:s + half] += part * on

    def compute(now):
        def one(t, carry):
            for r in range(rt_n):
                top = k * rt_n + r
                due = (t <= top) & (jnp.maximum(d_tick(t), f_tick(t, r)) == now)
                pl.when(due & (t < top))(lambda r=r: product(t, r, False))
                pl.when(due & (t == top))(lambda r=r: product(t, r, True))
            return carry

        lax.fori_loop(0, scens * rt_n, one, 0)

    def take(q):
        when(0 <= q < f_n + x_n, lambda: c_has(q, 1 - c), lambda: c_copy(q, 1 - c).wait_recv())

    def tick(now):
        n, m = now + rt_n - 1, now - 1

        def d_arrived():
            z_copy(n, True).wait_recv()
            forward_d(n)

        def x_arrived():
            x_copy(m, False).wait_recv()
            c_copy(m + f_n, c).start()

        when(now >= 1 and n < z_n, lambda: d_has(n, y), d_arrived)
        when(0 <= m < x_n, lambda: x_has(m, False), x_arrived)
        when(0 <= m < x_n, lambda: x_has(m, True), lambda: x_copy(m, True).wait_send())
        if now >= 1:
            send_x(now + 1)
        when(
            0 <= m < z_n, lambda: d_has(m, 1 - y), lambda: y_copy(m, True).wait_recv()
        )
        if now == 1:
            for q in range(f_n):
                take(q)
        if now >= 2:
            take(f_n + now - 2)
        compute(now)

    for now in range(max(z_n + 1, x_n + 2, 2)):
        tick(now)

    for r in range(rt_n):
        out[:, r * tile:(r + 1) * tile] = acc[r].astype(out.dtype)

    def drain_d(n):
        if n + rt_n < z_n:
            pl.when(d_has(n, y) & (z < levels - 1))(lambda: z_copy(n, False).wait_send())
        pl.when(y_sends(n))(lambda: y_copy(n, False).wait_send())

    for n in range(z_n):
        drain_d(n)

    def drain_c(q):
        pl.when(c_has(q, c))(lambda: c_copy(q, c).wait_send())

    for q in range(f_n + x_n):
        drain_c(q)


def local(scens, blks, draws, factor, occupancy):
    count, rows = draws.shape
    cols = factor.shape[1]
    tile = rows * scens // occupancy.shape[0]
    tiles = occupancy.shape[0]
    rt_n, ct_n = rows // tile, cols // tile
    z_n, f_n = scens // 2 * rt_n, rt_n * ct_n
    x_n = (blks // 2 - 1) * f_n
    dma = pltpu.SemaphoreType.DMA
    return pl.pallas_call(
        functools.partial(kernel, tile, scens, blks),
        out_shape=jax.ShapeDtypeStruct((count, rows), jnp.bfloat16),
        in_specs=[
            pl.BlockSpec(memory_space=pltpu.HBM),
            pl.BlockSpec(memory_space=pltpu.HBM),
            pl.BlockSpec(memory_space=pltpu.VMEM),
        ],
        out_specs=pl.BlockSpec(memory_space=pltpu.VMEM),
        scratch_shapes=[
            pltpu.VMEM((tiles, count, tile), jnp.bfloat16),
            pltpu.VMEM((tiles, rt_n, tile, tile), jnp.bfloat16),
            pltpu.VMEM((rt_n, count, tile), jnp.float32),
            dma((z_n,)), dma((z_n,)), dma((z_n,)), dma((z_n,)),
            dma((x_n,)), dma((x_n,)), dma((f_n + x_n,)), dma((f_n + x_n,)),
            dma((rt_n,)), dma((f_n,)),
        ],
        compiler_params=pltpu.CompilerParams(
            collective_id=0, has_side_effects=True, vmem_limit_bytes=48 * 1024 * 1024
        ),
        cost_estimate=pl.CostEstimate(
            flops=count * rows * rows * scens, bytes_accessed=8 * 1024 * 1024, transcendentals=0
        ),
    )(draws, factor, occupancy)


def solution(mesh):
    return jax.shard_map(
        functools.partial(local, mesh.shape["scen"], mesh.shape["blk"]),
        mesh=mesh,
        in_specs=(P("blk", "scen"), P("scen", "blk"), P()),
        out_specs=P("blk", "scen"),
        check_vma=False,
    )
```

```python
import functools

import jax
import jax.numpy as jnp
from jax import lax
from jax.experimental import pallas as pl
from jax.experimental.pallas import tpu as pltpu
from jax.sharding import PartitionSpec as P

MESH = pl.DeviceIdType.MESH


def kernel(
    tile, scens, blks,
    draws, factor, occ, out,
    dbuf, fbuf, acc,
    zsend, zrecv, ysend, yrecv, xsend, xrecv, csend, crecv, esend, erecv, dload, fload,
):
    levels, groups = scens // 2, blks // 2
    rows, cols = factor.shape
    rt_n, ct_n = rows // tile, cols // tile
    half = draws.shape[0] // 2
    z_n = levels * rt_n
    f_n = rt_n * ct_n
    x_n = (groups - 1) * f_n
    k = lax.axis_index("scen")
    b = lax.axis_index("blk")
    z, y = k // 2, k % 2
    x, c = b // 2, b % 2

    def d_tile(n, col):
        return ((z - n // rt_n) * 2 + col) * rt_n + n % rt_n

    def d_has(n, col):
        lev = z - n // rt_n
        return (n >= 0) & (n < z_n) & (lev >= 0) & (lev * 2 + col <= k)

    def when(inside, cond, body):
        if inside:
            pl.when(cond())(body)

    def z_copy(n, recv):
        t = d_tile(n, y)
        i = n if recv else n + rt_n
        return pltpu.make_async_remote_copy(
            src_ref=dbuf.at[t], dst_ref=dbuf.at[t],
            send_sem=zsend.at[n], recv_sem=zrecv.at[i],
            device_id=(k + 2, b), device_id_type=MESH,
        )

    def y_copy(n, recv):
        t = d_tile(n, 1 - y if recv else y)
        return pltpu.make_async_remote_copy(
            src_ref=dbuf.at[t], dst_ref=dbuf.at[t],
            send_sem=ysend.at[n], recv_sem=yrecv.at[n],
            device_id=(z * 2 + 1 - y, b), device_id_type=MESH,
        )

    early = rt_n > 1 and levels > 1

    def y_has(n, col):
        has = d_has(n, col)
        if early and n % rt_n == rt_n - 1:
            has &= (col == 1) | (z == 0) | (n // rt_n != z)
        return has

    def y_sends(n):
        return y_has(n, y) & ((y == 0) | (n >= rt_n))

    def e_copy():
        t = rt_n - 1
        return pltpu.make_async_remote_copy(
            src_ref=dbuf.at[t], dst_ref=dbuf.at[t],
            send_sem=esend.at[0], recv_sem=erecv.at[0],
            device_id=(k + 2, b), device_id_type=MESH,
        )

    def f_at(owner, f):
        return owner * ct_n + (ct_n - 1 - f // rt_n), f % rt_n

    def f_has(owner, f):
        t, r = f_at(owner, f)
        return t <= k * rt_n + r

    def x_owner(m, sending):
        step = m // f_n + 1
        other = lax.rem(x + step, groups) if sending else lax.rem(x + groups - step, groups)
        return other * 2 + c

    def x_copy(m, sending):
        f = m % f_n
        peer = x_owner(m, sending)
        t, r = f_at(b if sending else peer, f)
        return pltpu.make_async_remote_copy(
            src_ref=fbuf.at[t, r], dst_ref=fbuf.at[t, r],
            send_sem=xsend.at[m], recv_sem=xrecv.at[m],
            device_id=(k, peer), device_id_type=MESH,
        )

    def x_has(m, sending):
        return (m >= 0) & (m < x_n) & f_has(b if sending else x_owner(m, sending), m % f_n)

    def c_owner(q, core):
        m = q - f_n
        step = m // f_n + 1
        other = lax.rem(x + groups - step, groups)
        return jnp.where(q < f_n, x, other) * 2 + core

    def c_copy(q, core):
        t, r = f_at(c_owner(q, core), q % f_n)
        return pltpu.make_async_remote_copy(
            src_ref=fbuf.at[t, r], dst_ref=fbuf.at[t, r],
            send_sem=csend.at[q], recv_sem=crecv.at[q],
            device_id=(k, x * 2 + 1 - c), device_id_type=MESH,
        )

    def c_has(q, core):
        return (q >= 0) & (q < f_n + x_n) & f_has(c_owner(q, core), q % f_n)

    def d_load(h):
        return pltpu.make_async_copy(
            draws.at[:, pl.ds(h * tile, tile)], dbuf.at[k * rt_n + h], dload.at[h]
        )

    def f_load(f):
        t, r = f_at(b, f)
        lt = ct_n - 1 - f // rt_n
        return pltpu.make_async_copy(
            factor.at[pl.ds(r * tile, tile), pl.ds(lt * tile, tile)],
            fbuf.at[t, r],
            fload.at[f],
        )

    for h in range(rt_n):
        d_load(h).start()

    def load_f(f):
        @pl.when(f_has(b, f))
        def _():
            f_load(f).start()

    for f in range(f_n):
        load_f(f)

    barrier = pltpu.get_barrier_semaphore()

    def greet(kk, bb):
        pl.semaphore_signal(barrier, inc=1, device_id=(kk, bb), device_id_type=MESH)

    greet(z * 2 + 1 - y, b)
    greet(k, x * 2 + 1 - c)
    for step in range(1, groups):
        greet(k, lax.rem(x + step, groups) * 2 + c)

    @pl.when(z > 0)
    def _():
        greet(k - 2, b)

    @pl.when(z < levels - 1)
    def _():
        greet(k + 2, b)

    ends = jnp.where(z > 0, 1, 0) + jnp.where(z < levels - 1, 1, 0)
    pl.semaphore_wait(barrier, groups + 1 + ends)

    def forward_d(n):
        if n + rt_n < z_n:
            pl.when(z < levels - 1)(lambda: z_copy(n, False).start())
        pl.when(y_sends(n))(lambda: y_copy(n, False).start())

    def send_x(m):
        when(0 <= m < x_n, lambda: x_has(m, True), lambda: x_copy(m, True).start())

    for h in range(rt_n):
        d_load(h).wait()
        forward_d(h)

    def wait_f(f):
        @pl.when(f_has(b, f))
        def _():
            f_load(f).wait()

    for f in range(f_n):
        wait_f(f)
        if f < 2:
            send_x(f)
    for m in range(f_n, 2):
        send_x(m)

    def give_own(q):
        pl.when(c_has(q, c))(lambda: c_copy(q, c).start())

    for q in range(f_n):
        give_own(q)

    acc[...] = jnp.zeros_like(acc)

    def d_tick(t):
        owner, h = t // rt_n, t % rt_n
        lev, col = owner // 2, owner % 2
        n = (z - lev) * rt_n + h
        same = jnp.where(lev == z, 0, n - rt_n + 1)
        due = jnp.where(col == y, same, n + 1)
        if early:
            due = jnp.where((t == rt_n - 1) & (y == 1) & (z > 0), z * rt_n + 1, due)
        return due

    def f_tick(t, r):
        owner = t // ct_n
        f = (ct_n - 1 - t % ct_n) * rt_n + r
        ox, oc = owner // 2, owner % 2
        m = (lax.rem(x - ox + groups, groups) - 1) * f_n + f
        near = jnp.where(oc == c, 0, 1)
        far = jnp.where(oc == c, m + 1, m + 2)
        return jnp.where(ox == x, near, far)

    def product(t, r, masked):
        block = fbuf[t, r]
        if masked:
            row = lax.broadcasted_iota(jnp.int32, block.shape, 0)
            col = lax.broadcasted_iota(jnp.int32, block.shape, 1)
            block = jnp.where(col <= row, block.astype(jnp.float32), 0.0).astype(block.dtype)
        at_row = lax.broadcasted_iota(jnp.int32, occ.shape, 0) == k * rt_n + r
        at_col = lax.broadcasted_iota(jnp.int32, occ.shape, 1) == t
        mark = jnp.where(at_row & at_col, occ[...].astype(jnp.float32), 0.0)
        on = jnp.sum(jnp.sum(mark, axis=1, keepdims=True), axis=0, keepdims=True)
        for s in range(0, draws.shape[0], half):
            part = lax.dot_general(
                dbuf[t, s:s + half], block, (((1,), (1,)), ((), ())),
                preferred_element_type=jnp.float32,
            )
            acc[r, s:s + half] += part * on

    def compute(now):
        def one(t, carry):
            for r in range(rt_n):
                top = k * rt_n + r
                due = (t <= top) & (jnp.maximum(d_tick(t), f_tick(t, r)) == now)
                pl.when(due & (t < top))(lambda r=r: product(t, r, False))
                pl.when(due & (t == top))(lambda r=r: product(t, r, True))
            return carry

        lax.fori_loop(0, scens * rt_n, one, 0)

    def take(q):
        when(0 <= q < f_n + x_n, lambda: c_has(q, 1 - c), lambda: c_copy(q, 1 - c).wait_recv())

    def tick(now):
        n, m = now + rt_n - 1, now - 1

        def d_arrived():
            z_copy(n, True).wait_recv()
            forward_d(n)

        def e_arrived():
            e_copy().wait_recv()
            pl.when(z < levels - 1)(lambda: e_copy().start())

        def x_arrived():
            x_copy(m, False).wait_recv()
            c_copy(m + f_n, c).start()

        when(now >= 1 and n < z_n, lambda: d_has(n, y), d_arrived)
        when(0 <= m < x_n, lambda: x_has(m, False), x_arrived)
        when(0 <= m < x_n, lambda: x_has(m, True), lambda: x_copy(m, True).wait_send())
        if now >= 1:
            send_x(now + 1)
        if early:
            pl.when((y == 1) & (z > 0) & (z * rt_n + 1 == now))(e_arrived)
        when(
            0 <= m < z_n, lambda: y_has(m, 1 - y), lambda: y_copy(m, True).wait_recv()
        )
        if early and m == rt_n - 1:
            pl.when((y == 1) & (z == 0))(lambda: e_copy().start())
        if now == 1:
            for q in range(f_n):
                take(q)
        if now >= 2:
            take(f_n + now - 2)
        compute(now)

    for now in range(max(z_n + 1, x_n + 2, 2)):
        tick(now)

    for r in range(rt_n):
        out[:, r * tile:(r + 1) * tile] = acc[r].astype(out.dtype)

    def drain_d(n):
        if n + rt_n < z_n:
            pl.when(d_has(n, y) & (z < levels - 1))(lambda: z_copy(n, False).wait_send())
        pl.when(y_sends(n))(lambda: y_copy(n, False).wait_send())

    for n in range(z_n):
        drain_d(n)

    if early:
        pl.when((y == 1) & (z < levels - 1))(lambda: e_copy().wait_send())

    def drain_c(q):
        pl.when(c_has(q, c))(lambda: c_copy(q, c).wait_send())

    for q in range(f_n + x_n):
        drain_c(q)


def local(scens, blks, draws, factor, occupancy):
    count, rows = draws.shape
    cols = factor.shape[1]
    tile = rows * scens // occupancy.shape[0]
    tiles = occupancy.shape[0]
    rt_n, ct_n = rows // tile, cols // tile
    z_n, f_n = scens // 2 * rt_n, rt_n * ct_n
    x_n = (blks // 2 - 1) * f_n
    dma = pltpu.SemaphoreType.DMA
    return pl.pallas_call(
        functools.partial(kernel, tile, scens, blks),
        out_shape=jax.ShapeDtypeStruct((count, rows), jnp.bfloat16),
        in_specs=[
            pl.BlockSpec(memory_space=pltpu.HBM),
            pl.BlockSpec(memory_space=pltpu.HBM),
            pl.BlockSpec(memory_space=pltpu.VMEM),
        ],
        out_specs=pl.BlockSpec(memory_space=pltpu.VMEM),
        scratch_shapes=[
            pltpu.VMEM((tiles, count, tile), jnp.bfloat16),
            pltpu.VMEM((tiles, rt_n, tile, tile), jnp.bfloat16),
            pltpu.VMEM((rt_n, count, tile), jnp.float32),
            dma((z_n,)), dma((z_n,)), dma((z_n,)), dma((z_n,)),
            dma((x_n,)), dma((x_n,)), dma((f_n + x_n,)), dma((f_n + x_n,)),
            dma((1,)), dma((1,)), dma((rt_n,)), dma((f_n,)),
        ],
        compiler_params=pltpu.CompilerParams(
            collective_id=0, has_side_effects=True, vmem_limit_bytes=48 * 1024 * 1024
        ),
        cost_estimate=pl.CostEstimate(
            flops=count * rows * rows * scens, bytes_accessed=8 * 1024 * 1024, transcendentals=0
        ),
    )(draws, factor, occupancy)


def solution(mesh):
    return jax.shard_map(
        functools.partial(local, mesh.shape["scen"], mesh.shape["blk"]),
        mesh=mesh,
        in_specs=(P("blk", "scen"), P("scen", "blk"), P()),
        out_specs=P("blk", "scen"),
        check_vma=False,
    )
```

```python
import functools

import jax
import jax.numpy as jnp
from jax import lax
from jax.experimental import pallas as pl
from jax.experimental.pallas import tpu as pltpu
from jax.sharding import PartitionSpec as P

MESH = pl.DeviceIdType.MESH


def kernel(
    tile, scens, blks, skip,
    draws, factor, occ, out,
    dbuf, fbuf, acc,
    zsend, zrecv, ysend, yrecv, xsend, xrecv, csend, crecv, esend, erecv, dload, fload,
    pbuf, rbuf, codes,
):
    levels, groups = scens // 2, blks // 2
    rows, cols = factor.shape
    rt_n, ct_n = rows // tile, cols // tile
    half = draws.shape[0] // 2
    z_n = levels * rt_n
    f_n = rt_n * ct_n
    x_n = (groups - 1) * f_n - skip
    k = lax.axis_index("scen")
    b = lax.axis_index("blk")
    z, y = k // 2, k % 2
    x, c = b // 2, b % 2

    def d_tile(n, col):
        return ((z - n // rt_n) * 2 + col) * rt_n + n % rt_n

    def d_has(n, col):
        lev = z - n // rt_n
        return (n >= 0) & (n < z_n) & (lev >= 0) & (lev * 2 + col <= k)

    def when(inside, cond, body):
        if inside:
            pl.when(cond())(body)

    def z_copy(n, recv):
        t = d_tile(n, y)
        i = n if recv else n + rt_n
        return pltpu.make_async_remote_copy(
            src_ref=dbuf.at[t], dst_ref=dbuf.at[t],
            send_sem=zsend.at[n], recv_sem=zrecv.at[i],
            device_id=(k + 2, b), device_id_type=MESH,
        )

    def y_copy(n, recv):
        t = d_tile(n, 1 - y if recv else y)
        return pltpu.make_async_remote_copy(
            src_ref=dbuf.at[t], dst_ref=dbuf.at[t],
            send_sem=ysend.at[n], recv_sem=yrecv.at[n],
            device_id=(z * 2 + 1 - y, b), device_id_type=MESH,
        )

    early = rt_n > 1 and levels > 1

    def y_has(n, col):
        has = d_has(n, col)
        if early and n % rt_n == rt_n - 1:
            has &= (col == 1) | (z == 0) | (n // rt_n != z)
        return has

    def y_sends(n):
        return y_has(n, y) & ((y == 0) | (n >= rt_n))

    def e_copy():
        t = rt_n - 1
        return pltpu.make_async_remote_copy(
            src_ref=dbuf.at[t], dst_ref=dbuf.at[t],
            send_sem=esend.at[0], recv_sem=erecv.at[0],
            device_id=(k + 2, b), device_id_type=MESH,
        )

    def f_at(owner, f):
        return owner * ct_n + (ct_n - 1 - f // rt_n), f % rt_n

    def f_has(owner, f):
        t, r = f_at(owner, f)
        return t <= k * rt_n + r

    def x_owner(m, sending):
        step = m // f_n + 1
        other = lax.rem(x + step, groups) if sending else lax.rem(x + groups - step, groups)
        return other * 2 + c

    def x_copy(m, sending):
        if skip:
            return pltpu.make_async_remote_copy(
                src_ref=pbuf.at[m], dst_ref=rbuf.at[0, m],
                send_sem=xsend.at[m], recv_sem=xrecv.at[m],
                device_id=(k, (1 - x) * 2 + c), device_id_type=MESH,
            )
        f = m % f_n
        peer = x_owner(m, sending)
        t, r = f_at(b if sending else peer, f)
        return pltpu.make_async_remote_copy(
            src_ref=fbuf.at[t, r], dst_ref=fbuf.at[t, r],
            send_sem=xsend.at[m], recv_sem=xrecv.at[m],
            device_id=(k, peer), device_id_type=MESH,
        )

    def slot_has(owner, m):
        has = f_has(owner, m)
        for j in range(1, skip + 1):
            has |= f_has(owner, m + j)
        return has

    def x_has(m, sending):
        if skip:
            return slot_has(b if sending else (1 - x) * 2 + c, m)
        return (m >= 0) & (m < x_n) & f_has(b if sending else x_owner(m, sending), m % f_n)

    def c_owner(q, core):
        m = q - f_n
        step = m // f_n + 1
        other = lax.rem(x + groups - step, groups)
        return jnp.where(q < f_n, x, other) * 2 + core

    def c_copy(q, core):
        if skip and q >= f_n:
            return pltpu.make_async_remote_copy(
                src_ref=rbuf.at[0, q - f_n], dst_ref=rbuf.at[1, q - f_n],
                send_sem=csend.at[q], recv_sem=crecv.at[q],
                device_id=(k, x * 2 + 1 - c), device_id_type=MESH,
            )
        t, r = f_at(c_owner(q, core), q % f_n)
        return pltpu.make_async_remote_copy(
            src_ref=fbuf.at[t, r], dst_ref=fbuf.at[t, r],
            send_sem=csend.at[q], recv_sem=crecv.at[q],
            device_id=(k, x * 2 + 1 - c), device_id_type=MESH,
        )

    def c_has(q, core):
        if skip and q >= f_n:
            return slot_has((1 - x) * 2 + core, q - f_n)
        return (q >= 0) & (q < f_n + x_n) & f_has(c_owner(q, core), q % f_n)

    def d_load(h):
        return pltpu.make_async_copy(
            draws.at[:, pl.ds(h * tile, tile)], dbuf.at[k * rt_n + h], dload.at[h]
        )

    def f_load(f):
        t, r = f_at(b, f)
        lt = ct_n - 1 - f // rt_n
        return pltpu.make_async_copy(
            factor.at[pl.ds(r * tile, tile), pl.ds(lt * tile, tile)],
            fbuf.at[t, r],
            fload.at[f],
        )

    for h in range(rt_n):
        d_load(h).start()

    def load_f(f):
        @pl.when(True if skip else f_has(b, f))
        def _():
            f_load(f).start()

    for f in range(f_n):
        load_f(f)

    barrier = pltpu.get_barrier_semaphore()

    def greet(kk, bb):
        pl.semaphore_signal(barrier, inc=1, device_id=(kk, bb), device_id_type=MESH)

    greet(z * 2 + 1 - y, b)
    greet(k, x * 2 + 1 - c)
    for step in range(1, groups):
        greet(k, lax.rem(x + step, groups) * 2 + c)

    @pl.when(z > 0)
    def _():
        greet(k - 2, b)

    @pl.when(z < levels - 1)
    def _():
        greet(k + 2, b)

    ends = jnp.where(z > 0, 1, 0) + jnp.where(z < levels - 1, 1, 0)
    pl.semaphore_wait(barrier, groups + 1 + ends)

    def forward_d(n):
        if n + rt_n < z_n:
            pl.when(z < levels - 1)(lambda: z_copy(n, False).start())
        pl.when(y_sends(n))(lambda: y_copy(n, False).start())

    def send_x(m):
        when(0 <= m < x_n, lambda: x_has(m, True), lambda: x_copy(m, True).start())

    def mark(row, t):
        at_row = lax.broadcasted_iota(jnp.int32, occ.shape, 0) == row
        at_col = lax.broadcasted_iota(jnp.int32, occ.shape, 1) == t
        kept = jnp.where(at_row & at_col, occ[...].astype(jnp.float32), 0.0)
        return jnp.sum(jnp.sum(kept, axis=1, keepdims=True), axis=0, keepdims=True)

    def mark_codes(o, owner):
        passed = jnp.zeros((1, 1), jnp.float32)
        for f in range(f_n):
            t, r = f_at(owner, f)
            after = jnp.minimum(passed + 1.0 - mark(k * rt_n + r, t), float(skip))
            code = jnp.where(after > passed, -1.0, f - after)
            codes[o, f] = jnp.broadcast_to(code, codes.shape[2:])
            passed = after

    def in_slot(o, f, m):
        return jnp.broadcast_to(codes[o, f, 0:1, 0:1], (tile, tile)) == float(m)

    def pack(m):
        t, r = f_at(b, m)
        packed = fbuf[t, r].astype(jnp.float32)
        for j in range(1, skip + 1):
            t, r = f_at(b, m + j)
            packed = jnp.where(in_slot(0, m + j, m), fbuf[t, r].astype(jnp.float32), packed)
        pbuf[m] = packed.astype(pbuf.dtype)

    def unpack(m, via):
        owner = (1 - x) * 2 + jnp.where(via == 0, c, 1 - c)
        for j in range(skip + 1):
            f = m + j
            t, r = f_at(owner, f)
            if j == skip or m == 0:
                fbuf[t, r] = rbuf[via, m]
            else:
                new = rbuf[via, m].astype(jnp.float32)
                old = fbuf[t, r].astype(jnp.float32)
                fbuf[t, r] = jnp.where(in_slot(1 + via, f, m), new, old).astype(fbuf.dtype)

    for h in range(rt_n):
        d_load(h).wait()
        forward_d(h)

    def wait_f(f):
        @pl.when(True if skip else f_has(b, f))
        def _():
            f_load(f).wait()

    for f in range(f_n):
        wait_f(f)
        if f < 2 and not skip:
            send_x(f)
    if skip:
        mark_codes(0, b)
        for m in range(x_n):
            pack(m)
            if m < 2:
                send_x(m)
    for m in range(f_n, 2):
        send_x(m)

    def give_own(q):
        pl.when(c_has(q, c))(lambda: c_copy(q, c).start())

    for q in range(f_n):
        give_own(q)

    if skip:
        mark_codes(1, (1 - x) * 2 + c)
        mark_codes(2, (1 - x) * 2 + 1 - c)
    acc[...] = jnp.zeros_like(acc)

    def d_tick(t):
        owner, h = t // rt_n, t % rt_n
        lev, col = owner // 2, owner % 2
        n = (z - lev) * rt_n + h
        same = jnp.where(lev == z, 0, n - rt_n + 1)
        due = jnp.where(col == y, same, n + 1)
        if early:
            due = jnp.where((t == rt_n - 1) & (y == 1) & (z > 0), z * rt_n + 1, due)
        return due

    def f_tick(t, r):
        owner = t // ct_n
        f = (ct_n - 1 - t % ct_n) * rt_n + r
        ox, oc = owner // 2, owner % 2
        m = (lax.rem(x - ox + groups, groups) - 1) * f_n + f
        if skip:
            m = jnp.minimum(m, x_n - 1)
        near = jnp.where(oc == c, 0, 1)
        far = jnp.where(oc == c, m + 1, m + 2)
        return jnp.where(ox == x, near, far)

    def product(t, r, masked):
        block = fbuf[t, r]
        if masked:
            row = lax.broadcasted_iota(jnp.int32, block.shape, 0)
            col = lax.broadcasted_iota(jnp.int32, block.shape, 1)
            block = jnp.where(col <= row, block.astype(jnp.float32), 0.0).astype(block.dtype)
        on = mark(k * rt_n + r, t)
        for s in range(0, draws.shape[0], half):
            part = lax.dot_general(
                dbuf[t, s:s + half], block, (((1,), (1,)), ((), ())),
                preferred_element_type=jnp.float32,
            )
            acc[r, s:s + half] += part * on

    def compute(now):
        def one(t, carry):
            for r in range(rt_n):
                top = k * rt_n + r
                due = (t <= top) & (jnp.maximum(d_tick(t), f_tick(t, r)) == now)
                pl.when(due & (t < top))(lambda r=r: product(t, r, False))
                pl.when(due & (t == top))(lambda r=r: product(t, r, True))
            return carry

        lax.fori_loop(0, scens * rt_n, one, 0)

    def take(q):
        def taken():
            c_copy(q, 1 - c).wait_recv()
            if skip and q >= f_n:
                unpack(q - f_n, 1)

        when(0 <= q < f_n + x_n, lambda: c_has(q, 1 - c), taken)

    def tick(now):
        n, m = now + rt_n - 1, now - 1

        def d_arrived():
            z_copy(n, True).wait_recv()
            forward_d(n)

        def e_arrived():
            e_copy().wait_recv()
            pl.when(z < levels - 1)(lambda: e_copy().start())

        def x_arrived():
            x_copy(m, False).wait_recv()
            c_copy(m + f_n, c).start()

        when(now >= 1 and n < z_n, lambda: d_has(n, y), d_arrived)
        when(0 <= m < x_n, lambda: x_has(m, False), x_arrived)
        when(0 <= m < x_n, lambda: x_has(m, True), lambda: x_copy(m, True).wait_send())
        if now >= 1:
            send_x(now + 1)
        if early:
            pl.when((y == 1) & (z > 0) & (z * rt_n + 1 == now))(e_arrived)
        when(
            0 <= m < z_n, lambda: y_has(m, 1 - y), lambda: y_copy(m, True).wait_recv()
        )
        if early and m == rt_n - 1:
            pl.when((y == 1) & (z == 0))(lambda: e_copy().start())
        if now == 1:
            for q in range(f_n):
                take(q)
        if skip:
            when(0 <= m < x_n, lambda: x_has(m, False), lambda: unpack(m, 0))
        if now >= 2:
            take(f_n + now - 2)
        compute(now)

    for now in range(max(z_n + 1, x_n + 2, 2)):
        tick(now)

    for r in range(rt_n):
        out[:, r * tile:(r + 1) * tile] = acc[r].astype(out.dtype)

    def drain_d(n):
        if n + rt_n < z_n:
            pl.when(d_has(n, y) & (z < levels - 1))(lambda: z_copy(n, False).wait_send())
        pl.when(y_sends(n))(lambda: y_copy(n, False).wait_send())

    for n in range(z_n):
        drain_d(n)

    if early:
        pl.when((y == 1) & (z < levels - 1))(lambda: e_copy().wait_send())

    def drain_c(q):
        pl.when(c_has(q, c))(lambda: c_copy(q, c).wait_send())

    for q in range(f_n + x_n):
        drain_c(q)


def call(scens, blks, skip, draws, factor, occupancy):
    count, rows = draws.shape
    cols = factor.shape[1]
    tiles = occupancy.shape[0]
    tile = rows * scens // tiles
    rt_n, ct_n = rows // tile, cols // tile
    z_n, f_n = scens // 2 * rt_n, rt_n * ct_n
    x_n = (blks // 2 - 1) * f_n - skip
    slots = x_n if skip else 1
    side = tile if skip else 128
    dma = pltpu.SemaphoreType.DMA
    return pl.pallas_call(
        functools.partial(kernel, tile, scens, blks, skip),
        out_shape=jax.ShapeDtypeStruct((count, rows), jnp.bfloat16),
        in_specs=[
            pl.BlockSpec(memory_space=pltpu.HBM),
            pl.BlockSpec(memory_space=pltpu.HBM),
            pl.BlockSpec(memory_space=pltpu.VMEM),
        ],
        out_specs=pl.BlockSpec(memory_space=pltpu.VMEM),
        scratch_shapes=[
            pltpu.VMEM((tiles, count, tile), jnp.bfloat16),
            pltpu.VMEM((tiles, rt_n, tile, tile), jnp.bfloat16),
            pltpu.VMEM((rt_n, count, tile), jnp.float32),
            dma((z_n,)), dma((z_n,)), dma((z_n,)), dma((z_n,)),
            dma((x_n,)), dma((x_n,)), dma((f_n + x_n,)), dma((f_n + x_n,)),
            dma((1,)), dma((1,)), dma((rt_n,)), dma((f_n,)),
            pltpu.VMEM((slots, side, side), jnp.bfloat16),
            pltpu.VMEM((2, slots, side, side), jnp.bfloat16),
            pltpu.VMEM((3, f_n, 8, 128), jnp.float32),
        ],
        compiler_params=pltpu.CompilerParams(
            collective_id=skip, has_side_effects=True, vmem_limit_bytes=56 * 1024 * 1024
        ),
        cost_estimate=pl.CostEstimate(
            flops=count * rows * rows * scens, bytes_accessed=8 * 1024 * 1024, transcendentals=0
        ),
    )(draws, factor, occupancy)


def local(scens, blks, draws, factor, occupancy):
    tiles = occupancy.shape[0]
    rt_n, ct_n = tiles // scens, tiles // blks
    f_n = rt_n * ct_n
    most = 2 if blks == 4 and f_n >= 4 else 0
    whole = functools.partial(call, scens, blks, 0)
    if most == 0:
        return whole(draws, factor, occupancy)
    filled = jnp.max(jnp.sum(occupancy.reshape(scens, rt_n, blks, ct_n), axis=(1, 3)))
    forms = [whole] + [functools.partial(call, scens, blks, n) for n in range(1, most + 1)]
    return lax.switch(jnp.minimum(f_n - filled, most), forms, draws, factor, occupancy)


def solution(mesh):
    return jax.shard_map(
        functools.partial(local, mesh.shape["scen"], mesh.shape["blk"]),
        mesh=mesh,
        in_specs=(P("blk", "scen"), P("scen", "blk"), P()),
        out_specs=P("blk", "scen"),
        check_vma=False,
    )
```
